512 devices in a mesh: dp: 32 (over z, y_lo, core), ctx: 16 (over x, y_hi).
Axes of the slice: x: 4, y: 8 (y_hi: 4, y_lo: 2; y = y_hi * 2 + y_lo), z: 8, core: 2. Of those that a mesh axis runs over, the one named last changes fastest.
Arguments:
- queries: bfloat16 [32, 2048, 4096], P('dp', 'ctx'), may hold values from -100 to 100
- keys: bfloat16 [32, 2048, 512], P('dp', 'ctx'), may hold values from -6 to 6
- values: bfloat16 [32, 2048, 512], P('dp', 'ctx'), may hold values from -6 to 6
- out_cotangent: bfloat16 [32, 2048, 4096], P('dp', 'ctx'), may hold values from -6 to 6
- rewards: float32 [32, 6], P('dp'), may hold values from -18 to 18
- lengths: int32 [32, 6], P('dp'), may hold values from 1 to 5, 15 in all within a row
Outputs:
- attn_out: bfloat16 [32, 2048, 4096], P('dp', 'ctx')
- query_grad: bfloat16 [32, 2048, 4096], P('dp', 'ctx')
- key_grad: bfloat16 [32, 2048, 512], P('dp', 'ctx')
- value_grad: bfloat16 [32, 2048, 512], P('dp', 'ctx')
The draws below stay inside these ranges and needn't reach their ends.
Inputs may be any that keep to these rules, and one draw needn't show every extreme that they name: Each tree's response lengths, counted in blocks of 128 tokens, sum to 15, and the longest is exactly 5 blocks.
All inputs are finite; a program needn't handle non-finite values.
Results may differ from the reference program's by a relative error of at most 0.012.
Values may be sent and summed in bfloat16 or wider, within the bound.
A program may use at most 64 MiB of HBM per device.

```python
import math
import jax
import jax.numpy as jnp
import numpy as np
from jax import lax

H = 32
KVH = 4
HD = 128
BLOCK = 128
TREES = 32
SEQ = 2048
NBLK = 16
RESP = 6
MOST = 5


def key_field(key):
    return jax.random.truncated_normal(key, -6.0, 6.0, (TREES, SEQ, KVH * HD), jnp.float32)


def draw_keys(key, part):
    field = key_field(key)
    return field.astype(jnp.bfloat16)


def draw_queries(key, part):
    key = jax.random.fold_in(key, 7)
    first_key = jax.random.fold_in(key, 0)
    rows = jax.random.truncated_normal(first_key, -6.0, 6.0, (TREES, SEQ, H * HD), jnp.float32)
    return rows.astype(jnp.bfloat16)


def draw_rewards(key, part):
    key = jax.random.fold_in(key, 5)
    rising = jnp.arange(TREES, dtype=jnp.float32)[:, None] / max(TREES - 1, 1)
    field = jax.random.truncated_normal(key, -6.0, 6.0, (TREES, RESP), jnp.float32) * jnp.power(3.0, 0.5 * rising)
    return field


def block_levels(rng, extent, cuts, low, high):
    loudness = 1.0
    for dim, blocks in cuts:
        steps = jax.random.uniform(jax.random.fold_in(jax.random.fold_in(rng, 6), dim), (blocks,), jnp.float32, low / len(cuts), high / len(cuts))
        loudness = loudness * jnp.repeat(jnp.exp(steps), extent[dim] // blocks).reshape((-1,) + (1,) * (len(extent) - 1 - dim))
    return loudness


def length_profile(number_of, total, reach, lean):
    loads = [(1 << 20) // math.isqrt(rank ** lean) + 1 for rank in range(2, number_of + 1)]
    rest, counts = total - reach - (number_of - 1), [1] * (number_of - 1)
    while rest > 0:
        candidates = [i for i in range(number_of - 1) if counts[i] < reach]
        whole, budget = sum([loads[i] for i in candidates]), rest
        for i in candidates:
            addition = min(reach - counts[i], max(1, budget * loads[i] // whole), rest)
            counts[i] = counts[i] + addition
            rest = rest - addition
    return np.array([reach] + counts)


def uneven(own_key, number_of, total, reach, slope):
    if number_of == 2:
        one = jax.random.randint(own_key, (), max(1, total - reach), min(reach, total - 1) + 1)
        return jnp.stack([one, total - one])
    tallies = jnp.asarray(length_profile(number_of, total, reach, slope), jnp.int32)
    pairs = (number_of - 1) // 2
    source_of, sink = tallies[1:1 + 2 * pairs:2], tallies[2:2 + 2 * pairs:2]
    margin = jnp.minimum(source_of - 1, reach - sink)
    moved = jax.random.randint(jax.random.fold_in(own_key, 1), (pairs,), 0, 1 << 20) % (margin + 1)
    tallies = tallies.at[1:1 + 2 * pairs:2].set(source_of - moved).at[2:2 + 2 * pairs:2].set(sink + moved)
    return tallies[jax.random.permutation(jax.random.fold_in(own_key, 2), number_of)]


def scatter_about(rng, shape, width, reach, pieces=(), kind=jnp.bfloat16):
    values = jax.random.normal(rng, shape, jnp.float32) * width
    if len(pieces) > 0:
        values = block_levels(rng, shape, pieces, -0.22, 0.18) * values
    return jnp.clip(values, min=-reach, max=reach).astype(kind)


def setup_inputs(seed: int = 0) -> dict:
    seeds = jax.random.split(jax.random.key(seed), 7)
    queries = draw_queries(jax.random.fold_in(seeds[6], 71), 0)
    keys = draw_keys(jax.random.fold_in(seeds[6], 71), 0)
    values = scatter_about(seeds[2], (TREES, SEQ, KVH * HD), 1.0, 6.0, ((0, 32), (1, 16)))
    out_cotangent = scatter_about(seeds[3], (TREES, SEQ, H * HD), 1.0, 6.0, ((0, 32), (1, 16)))
    rewards = draw_rewards(jax.random.fold_in(seeds[6], 71), 0)
    lengths = jax.vmap(lambda own: uneven(own, RESP, NBLK - 1, MOST, 2))(jax.random.split(seeds[5], TREES)).reshape((TREES, RESP)).astype(jnp.int32)
    return dict(queries=queries, keys=keys, values=values, out_cotangent=out_cotangent, rewards=rewards, lengths=lengths)


def response_table(lengths_row):
    block_ends = jnp.cumsum(lengths_row)
    starts = (1 + block_ends - lengths_row).astype(jnp.int32)
    blocks = jnp.arange(NBLK, dtype=jnp.int32)
    inside = starts[None, :] <= blocks[:, None]
    first_block = lax.optimization_barrier(jnp.max(jnp.where(inside, starts[None, :], 1), axis=1)).astype(jnp.int32)
    return (first_block, starts)

def reference(queries, keys, values, out_cotangent, rewards, lengths):
    centered = rewards - lax.optimization_barrier(jnp.mean(rewards, axis=1, keepdims=True))
    spread = jnp.sum(centered * centered) / (TREES * RESP)
    advantage = centered / jnp.sqrt(spread + 1e-06)
    scale = HD ** (-0.5)
    ratio = H // KVH

    def one_group(group_args):
        query_part, key_part, value_part, cot_part, allowed = group_args
        q32 = query_part.astype(jnp.float32)
        k32 = key_part.astype(jnp.float32)
        v32 = value_part.astype(jnp.float32)
        c32 = cot_part.astype(jnp.float32)
        scores = jnp.einsum('igd,jd->gij', q32, k32) * scale
        scores = jnp.where(allowed[None], scores, -jnp.inf)
        peak = lax.optimization_barrier(jnp.max(scores, axis=2, keepdims=True))
        lse = peak + jnp.log(lax.optimization_barrier(jnp.sum(jnp.exp(scores - peak), axis=2, keepdims=True)))
        probs = jnp.exp(scores - lse)
        probs_low = probs.astype(jnp.bfloat16)
        attn = jnp.einsum('gij,jd->igd', probs_low.astype(jnp.float32), v32).astype(jnp.bfloat16)
        delta = lax.optimization_barrier(jnp.sum(c32 * attn.astype(jnp.float32), axis=2))
        dprobs = jnp.einsum('igd,jd->gij', c32, v32)
        dscores = (probs * (dprobs - delta.T[:, :, None]) * scale).astype(jnp.bfloat16)
        ds32 = dscores.astype(jnp.float32)
        qgrad = jnp.einsum('gij,jd->igd', ds32, k32).astype(jnp.bfloat16)
        kgrad = jnp.einsum('gij,igd->jd', ds32, q32).astype(jnp.bfloat16)
        vgrad = jnp.einsum('gij,igd->jd', probs_low.astype(jnp.float32), c32).astype(jnp.bfloat16)
        return (attn, qgrad, kgrad, vgrad)

    def one_tree(tree_args):
        query_tree, key_tree, value_tree, cot_tree, adv_row, lengths_row = tree_args
        first_block, starts = response_table(lengths_row)
        positions = jnp.arange(SEQ, dtype=jnp.int32)
        token_block = positions // BLOCK
        token_first = jnp.take(first_block, token_block)
        allowed = (positions[None, :] <= positions[:, None]) & ((token_block[None, :] == 0) | (token_first[None, :] == token_first[:, None]))
        owner_id = lax.optimization_barrier(jnp.sum((starts[None, :] <= token_block[:, None]).astype(jnp.int32), axis=1)) - 1
        weight = lax.optimization_barrier(jnp.sum(jnp.where(owner_id[:, None] == jnp.arange(RESP, dtype=jnp.int32)[None, :], adv_row[None, :], 0.0), axis=1))
        weighted = (weight[:, None] * cot_tree.astype(jnp.float32)).astype(jnp.bfloat16)
        query_four = jnp.moveaxis(query_tree.reshape(SEQ, KVH, ratio, HD), 1, 0)
        cot_four = jnp.moveaxis(weighted.reshape(SEQ, KVH, ratio, HD), 1, 0)
        key_three = jnp.moveaxis(key_tree.reshape(SEQ, KVH, HD), 1, 0)
        value_three = jnp.moveaxis(value_tree.reshape(SEQ, KVH, HD), 1, 0)
        allowed_all = jnp.broadcast_to(allowed[None], (KVH, SEQ, SEQ))
        attn, qgrad, kgrad, vgrad = lax.map(one_group, (query_four, key_three, value_three, cot_four, allowed_all))
        attn = jnp.moveaxis(attn, 0, 1).reshape(SEQ, H * HD)
        qgrad = jnp.moveaxis(qgrad, 0, 1).reshape(SEQ, H * HD)
        kgrad = jnp.moveaxis(kgrad, 0, 1).reshape(SEQ, KVH * HD)
        vgrad = jnp.moveaxis(vgrad, 0, 1).reshape(SEQ, KVH * HD)
        return (attn, qgrad, kgrad, vgrad)
    attn_out, query_grad, key_grad, value_grad = lax.map(one_tree, (queries, keys, values, out_cotangent, advantage, lengths))
    return (attn_out, query_grad, key_grad, value_grad)
```

```python
import functools

import jax
import jax.numpy as jnp
from jax import lax
from jax.experimental import pallas as pl
from jax.experimental.pallas import tpu as pltpu
from jax.sharding import PartitionSpec as P

H = 32
KVH = 4
HD = 128
BLOCK = 128
RESP = 6
BACK = 4
SLOTS = BACK + 2
OWN = SLOTS - 1
COLS = 4
QUAD = 4
RATIO = H // KVH
PAIRS = RATIO // 2
WIDE = 2 * BLOCK
SCALE = HD ** (-0.5)
LOG2E = 1.4426950408889634
MASKED = -1e30
MESH = pl.DeviceIdType.MESH
NT = (((1,), (1,)), ((), ()))
NN = (((1,), (0,)), ((), ()))


def dot(a, b, dims=NN):
    return lax.dot_general(a, b, dims, preferred_element_type=jnp.float32)


def kernel(
    ctx,
    dp,
    q_ref,
    c_ref,
    k_ref,
    v_ref,
    rew_ref,
    len_ref,
    o_ref,
    dq_ref,
    dk_ref,
    dv_ref,
    kv,
    kt,
    vt,
    acc,
    own,
    give,
    got,
    chain,
    stat,
    quad_got,
    line_got,
    fsend,
    frecv,
    rsend,
    gsend,
    grecv,
    csend,
    crecv,
    qsend,
    qrecv,
    lsend,
    lrecv,
):
    me = lax.axis_index("ctx")
    col = me // COLS
    last = ctx // COLS - 1
    my_dp = lax.axis_index("dp")
    quads = dp // QUAD

    barrier = pltpu.get_barrier_semaphore()

    def greet_ctx(d, carry):
        pl.semaphore_signal(
            barrier, inc=1, device_id={"ctx": lax.rem(me + d, ctx)}, device_id_type=MESH
        )
        return carry

    lax.fori_loop(1, ctx, greet_ctx, 0)
    greeted = ctx - 1
    quad_base = my_dp // QUAD * QUAD
    quad_at = my_dp - quad_base

    def quad_peer(d):
        return quad_base + lax.rem(quad_at + d, QUAD)

    def line_peer(d):
        return lax.rem(my_dp // QUAD + d, quads) * QUAD + quad_at

    if dp > 1:
        for d in range(1, QUAD):
            pl.semaphore_signal(barrier, inc=1, device_id={"dp": quad_peer(d)}, device_id_type=MESH)
        for d in range(1, quads):
            pl.semaphore_signal(barrier, inc=1, device_id={"dp": line_peer(d)}, device_id_type=MESH)
        greeted += QUAD - 1 + quads - 1

    for g in range(KVH):
        kv[g, OWN, 0] = k_ref[:, g * HD : (g + 1) * HD]
        kv[g, OWN, 1] = v_ref[:, g * HD : (g + 1) * HD]

    def blank(slot):
        for g in range(KVH):
            kv[g, slot] = jnp.zeros((2, BLOCK, HD), jnp.bfloat16)

    @pl.when(me == 0)
    def _():
        blank(0)

    for k in range(1, BACK + 1):

        @pl.when(me <= k)
        def _():
            blank(OWN - k)

    mean = rew_ref[0, 0]
    for r in range(1, RESP):
        mean = mean + rew_ref[0, r]
    mean = mean * (1.0 / RESP)
    square = jnp.float32(0.0)
    advantage = jnp.float32(0.0)
    first = jnp.int32(1)
    start = jnp.int32(1)
    for r in range(RESP):
        centered = rew_ref[0, r] - mean
        square = square + centered * centered
        advantage = jnp.where(start <= me, centered, advantage)
        first = jnp.where(start <= me, start, first)
        start = start + len_ref[0, r]
    stat[0] = jnp.full((8, HD), square, jnp.float32)
    bias = [jnp.where(me >= 1, 0.0, MASKED).astype(jnp.float32)]
    for k in range(BACK, 0, -1):
        bias.append(jnp.where(me - k >= first, 0.0, MASKED).astype(jnp.float32))

    pl.semaphore_wait(barrier, greeted)

    def key_copy(g, src_slot, dst_slot, send, target):
        return pltpu.make_async_remote_copy(
            src_ref=kv.at[g, src_slot],
            dst_ref=kv.at[g, dst_slot],
            send_sem=send,
            recv_sem=frecv.at[g, dst_slot],
            device_id={"ctx": target},
            device_id_type=MESH,
        )

    sends = [((me >= 1) & (me + k < ctx), k, OWN - k) for k in range(1, BACK + 1)]
    sends += [(me == 0, k, 0) for k in (1, 2, 3, COLS, last * COLS)]

    def each_send(g, do):
        for n, (when, distance, slot) in enumerate(sends):

            @pl.when(when)
            def _():
                do(key_copy(g, OWN, slot, fsend.at[g, n], lax.rem(me + distance, ctx)))

    def send_group(g, carry):
        each_send(g, lambda copy: copy.start())
        return carry

    lax.fori_loop(0, KVH, send_group, 0)

    relays = [
        ((me >= 1) & (me < 2 * COLS), COLS),
        ((me >= 1) & (me < COLS), last * COLS),
    ]

    def each_relay(g, do):
        for n, (when, distance) in enumerate(relays):
            if n == 0:
                when = when & (me + COLS < last * COLS)

            @pl.when(when)
            def _():
                do(key_copy(g, 0, 0, rsend.at[g, n], lax.rem(me + distance, ctx)))

    def take_prompt(g):
        @pl.when(me >= 1)
        def _():
            key_copy(g, OWN, 0, fsend.at[g, 0], lax.rem(me + 1, ctx)).wait_recv()

        each_relay(g, lambda copy: copy.start())

    def share(src, dst, send, recv, target):
        return pltpu.make_async_remote_copy(
            src_ref=src,
            dst_ref=dst,
            send_sem=send,
            recv_sem=recv,
            device_id={"dp": target},
            device_id_type=MESH,
        )

    def quad_copy(d):
        return share(
            stat.at[0], quad_got.at[d - 1], qsend.at[d - 1], qrecv.at[d - 1], quad_peer(d)
        )

    def line_copy(d):
        return share(
            stat.at[1], line_got.at[d - 1], lsend.at[d - 1], lrecv.at[d - 1], line_peer(d)
        )

    if dp > 1:
        for d in range(1, QUAD):
            quad_copy(d).start()
        for d in range(1, QUAD):
            quad_copy(d).wait()
        part = stat[0]
        for d in range(1, QUAD):
            part = part + quad_got[d - 1]
        stat[1] = part
        for d in range(1, quads):
            line_copy(d).start()
    take_prompt(0)
    if dp > 1:
        for d in range(1, quads):
            line_copy(d).wait()
        total = stat[1]
        for d in range(1, quads):
            total = total + line_got[d - 1]
    else:
        total = stat[0]
    weight = advantage * SCALE / jnp.sqrt(total * (1.0 / (dp * RESP)) + 1e-06)
    stat[0] = weight

    def grad_copy(g, k):
        return pltpu.make_async_remote_copy(
            src_ref=give.at[g, OWN - k],
            dst_ref=got.at[g, k - 1],
            send_sem=gsend.at[g, k - 1],
            recv_sem=grecv.at[g, k - 1],
            device_id={"ctx": lax.rem(me + ctx - k, ctx)},
            device_id_type=MESH,
        )

    def each_grad(g, do):
        for k in range(1, BACK + 1):

            @pl.when(me > k)
            def _():
                do(grad_copy(g, k))

    def chain_copy(g, n, distance):
        return pltpu.make_async_remote_copy(
            src_ref=give.at[g, 0],
            dst_ref=chain.at[g, n],
            send_sem=csend.at[g],
            recv_sem=crecv.at[g, n],
            device_id={"ctx": lax.rem(me + ctx - distance, ctx)},
            device_id_type=MESH,
        )

    def home_copy(g, k):
        return pltpu.make_async_remote_copy(
            src_ref=give.at[g, 0],
            dst_ref=got.at[g, k - 1],
            send_sem=csend.at[g],
            recv_sem=grecv.at[g, k - 1],
            device_id={"ctx": lax.rem(me + ctx - k, ctx)},
            device_id_type=MESH,
        )

    in_first = (me >= 1) & (me < COLS)
    in_second = (me >= COLS) & (me < 2 * COLS)
    in_third = (me >= 2 * COLS) & (me < last * COLS)
    in_last = me >= last * COLS

    def chain_ends(g, do):
        @pl.when(in_third)
        def _():
            do(chain_copy(g, 0, COLS))

        @pl.when(in_last)
        def _():
            do(chain_copy(g, 1, last * COLS))

    def chain_middle(g):
        @pl.when(in_second)
        def _():
            chain_copy(g, 0, COLS).wait_recv()
            give[g, 0] = (
                give[g, 0].astype(jnp.float32) + chain[g, 0].astype(jnp.float32)
            ).astype(jnp.bfloat16)
            chain_copy(g, 0, COLS).start()

    def chain_home(g):
        @pl.when(in_first)
        def _():
            chain_copy(g, 0, COLS).wait_recv()
            chain_copy(g, 1, COLS).wait_recv()
            give[g, 0] = (
                give[g, 0].astype(jnp.float32)
                + chain[g, 0].astype(jnp.float32)
                + chain[g, 1].astype(jnp.float32)
            ).astype(jnp.bfloat16)
            for k in range(1, COLS):

                @pl.when(me == k)
                def _():
                    home_copy(g, k).start()

    row = lax.broadcasted_iota(jnp.int32, (BLOCK, WIDE), 0)
    column = lax.broadcasted_iota(jnp.int32, (BLOCK, WIDE), 1)
    causal = row <= lax.rem(column, BLOCK)

    def pair_step(g, pair):
        base = pl.multiple_of(g * (RATIO * HD) + pair * WIDE, WIDE)
        left = pl.ds(base, HD)
        right = pl.ds(pl.multiple_of(base + HD, HD), HD)
        query = jnp.concatenate([q_ref[:, left], q_ref[:, right]], axis=0)
        cot = jnp.concatenate([c_ref[:, left], c_ref[:, right]], axis=0)
        keys = kv[g, :, 0].reshape(SLOTS * BLOCK, HD)
        values = kv[g, :, 1].reshape(SLOTS * BLOCK, HD)
        raw = dot(keys, query, NT) * (SCALE * LOG2E)
        tiles = [raw[s * BLOCK : (s + 1) * BLOCK] + bias[s] for s in range(OWN)]
        tiles.append(jnp.where(causal, raw[OWN * BLOCK :], MASKED))
        scores = jnp.concatenate(tiles, axis=0)
        peak = jnp.max(scores, axis=0, keepdims=True)
        exps = jnp.exp2(scores - peak)
        probs = exps * (1.0 / jnp.sum(exps, axis=0, keepdims=True))
        low = probs.astype(jnp.bfloat16)
        dprobs = dot(values, cot, NT)
        delta = jnp.sum(probs * dprobs, axis=0, keepdims=True)
        dscores = (probs * (dprobs - delta)).astype(jnp.bfloat16)
        attn = dot(vt[...], low)
        qgrad = dot(kt[...], dscores) * stat[0, 0:1, 0:1]
        acc[0] += dot(dscores, query)
        acc[1] += dot(low, cot)
        o_ref[:, left] = attn[:, :HD].T.astype(jnp.bfloat16)
        o_ref[:, right] = attn[:, HD:].T.astype(jnp.bfloat16)
        dq_ref[:, left] = qgrad[:, :HD].T.astype(jnp.bfloat16)
        dq_ref[:, right] = qgrad[:, HD:].T.astype(jnp.bfloat16)

    def group_step(g, carry):
        for k in range(1, BACK + 1):

            @pl.when(me > k)
            def _():
                key_copy(g, OWN, OWN - k, fsend.at[g, 0], lax.rem(me + 1, ctx)).wait_recv()

        kt[...] = kv[g, :, 0].reshape(SLOTS * BLOCK, HD).T
        vt[...] = kv[g, :, 1].reshape(SLOTS * BLOCK, HD).T
        acc[...] = jnp.zeros_like(acc)

        def pairs(pair, inner):
            pair_step(g, pair)
            return inner

        lax.fori_loop(0, PAIRS // 2, pairs, 0)

        @pl.when(g < KVH - 1)
        def _():
            take_prompt(g + 1)

        @pl.when(g > 0)
        def _():
            chain_middle(g - 1)

        lax.fori_loop(PAIRS // 2, PAIRS, pairs, 0)

        scale = stat[0, 0:1, :]
        for s in range(OWN):
            rows = pl.ds(s * BLOCK, BLOCK)
            give[g, s, 0] = (acc[0, rows, :] * scale).astype(jnp.bfloat16)
            give[g, s, 1] = (acc[1, rows, :] * (scale * (1.0 / SCALE))).astype(jnp.bfloat16)
        rows = pl.ds(OWN * BLOCK, BLOCK)
        own[g, 0] = acc[0, rows, :] * scale
        own[g, 1] = acc[1, rows, :] * (scale * (1.0 / SCALE))
        each_grad(g, lambda copy: copy.start())
        chain_ends(g, lambda copy: copy.start())

        @pl.when(g > 0)
        def _():
            chain_home(g - 1)

        return carry

    lax.fori_loop(0, KVH, group_step, 0)
    chain_middle(KVH - 1)
    chain_home(KVH - 1)

    def close_group(g, carry):
        def add(part):
            own[g] += part.astype(jnp.float32)

        for k in range(1, BACK + 1):
            here = (me >= 1) & (me + k < ctx)
            if k < COLS:
                here = here | (me == 0)

            @pl.when(here)
            def _():
                grad_copy(g, k).wait_recv()
                add(got[g, k - 1])

        @pl.when(me == 0)
        def _():
            for n in range(2):
                chain_copy(g, n, COLS).wait_recv()
                add(chain[g, n])

        at = pl.ds(pl.multiple_of(g * HD, HD), HD)
        dk_ref[:, at] = own[g, 0].astype(jnp.bfloat16)
        dv_ref[:, at] = own[g, 1].astype(jnp.bfloat16)
        return carry

    lax.fori_loop(0, KVH, close_group, 0)

    def settle(g, carry):
        each_send(g, lambda copy: copy.wait_send())
        each_relay(g, lambda copy: copy.wait_send())
        each_grad(g, lambda copy: copy.wait_send())

        @pl.when(me >= 1)
        def _():
            chain_copy(g, 0, COLS).wait_send()

        return carry

    lax.fori_loop(0, KVH, settle, 0)


def body(queries, keys, values, out_cotangent, rewards, lengths):
    ctx = lax.axis_size("ctx")
    dp = lax.axis_size("dp")
    tokens = queries.shape[1]
    vmem = pl.BlockSpec(memory_space=pltpu.VMEM)
    smem = pl.BlockSpec(memory_space=pltpu.SMEM)
    wide = jax.ShapeDtypeStruct((tokens, H * HD), jnp.bfloat16)
    thin = jax.ShapeDtypeStruct((tokens, KVH * HD), jnp.bfloat16)
    block = (2, BLOCK, HD)
    quads = max(dp // QUAD - 1, 1)
    dma = pltpu.SemaphoreType.DMA
    outs = pl.pallas_call(
        functools.partial(kernel, ctx, dp),
        out_shape=(wide, wide, thin, thin),
        in_specs=[vmem] * 4 + [smem] * 2,
        out_specs=(vmem,) * 4,
        scratch_shapes=[
            pltpu.VMEM((KVH, SLOTS) + block, jnp.bfloat16),
            pltpu.VMEM((HD, SLOTS * BLOCK), jnp.bfloat16),
            pltpu.VMEM((HD, SLOTS * BLOCK), jnp.bfloat16),
            pltpu.VMEM((2, SLOTS * BLOCK, HD), jnp.float32),
            pltpu.VMEM((KVH,) + block, jnp.float32),
            pltpu.VMEM((KVH, OWN) + block, jnp.bfloat16),
            pltpu.VMEM((KVH, BACK) + block, jnp.bfloat16),
            pltpu.VMEM((KVH, 2) + block, jnp.bfloat16),
            pltpu.VMEM((2, 8, HD), jnp.float32),
            pltpu.VMEM((QUAD - 1, 8, HD), jnp.float32),
            pltpu.VMEM((quads, 8, HD), jnp.float32),
            dma((KVH, BACK + 5)),
            dma((KVH, SLOTS)),
            dma((KVH, 2)),
            dma((KVH, BACK)),
            dma((KVH, BACK)),
            dma((KVH,)),
            dma((KVH, 2)),
            dma((QUAD - 1,)),
            dma((QUAD - 1,)),
            dma((quads,)),
            dma((quads,)),
        ],
        compiler_params=pltpu.CompilerParams(
            collective_id=0, has_side_effects=True, vmem_limit_bytes=48 * 1024 * 1024
        ),
        name="tree_attention",
    )(queries[0], out_cotangent[0], keys[0], values[0], rewards, lengths)
    return tuple(out[None] for out in outs)


def solution(mesh):
    placed = (P("dp", "ctx", None),) * 4
    return jax.shard_map(
        body,
        mesh=mesh,
        in_specs=placed + (P("dp", None),) * 2,
        out_specs=placed,
        check_vma=False,
    )
```

```python
import functools

import jax
import jax.numpy as jnp
from jax import lax
from jax.experimental import pallas as pl
from jax.experimental.pallas import tpu as pltpu
from jax.sharding import PartitionSpec as P

H = 32
KVH = 4
HD = 128
BLOCK = 128
RESP = 6
BACK = 4
SLOTS = BACK + 2
OWN = SLOTS - 1
COLS = 4
QUAD = 4
RATIO = H // KVH
PAIRS = RATIO // 2
WIDE = 2 * BLOCK
SCALE = HD ** (-0.5)
LOG2E = 1.4426950408889634
MASKED = -1e30
OUT_STRAIGHT = 1
BACK_STRAIGHT = 1
AHEAD = 2
FORCED = True
MESH = pl.DeviceIdType.MESH
NT = (((1,), (1,)), ((), ()))
NN = (((1,), (0,)), ((), ()))


def dot(a, b, dims=NN):
    return lax.dot_general(a, b, dims, preferred_element_type=jnp.float32)


def kernel(
    ctx,
    dp,
    q_hbm,
    c_hbm,
    k_hbm,
    v_hbm,
    rew_ref,
    len_ref,
    o_hbm,
    dq_hbm,
    dk_ref,
    dv_ref,
    o_ref,
    dq_ref,
    q_ref,
    c_ref,
    k_ref,
    v_ref,
    kv,
    kt,
    vt,
    acc,
    own,
    give,
    got,
    chain,
    help_got,
    stat,
    quad_got,
    line_got,
    load,
    store,
    fsend,
    frecv,
    rsend,
    gsend,
    grecv,
    hsend,
    hrecv,
    csend,
    crecv,
    qsend,
    qrecv,
    lsend,
    lrecv,
):
    me = lax.axis_index("ctx")
    end = ctx - 1
    my_dp = lax.axis_index("dp")
    quads = dp // QUAD
    upward = lax.rem(my_dp, 2) == 0

    loads = [
        pltpu.make_async_copy(src, dst, load.at[n])
        for n, (src, dst) in enumerate(
            ((k_hbm, k_ref), (v_hbm, v_ref), (q_hbm, q_ref), (c_hbm, c_ref))
        )
    ]
    for copy in loads:
        copy.start()

    barrier = pltpu.get_barrier_semaphore()

    def greet_ctx(d, carry):
        pl.semaphore_signal(
            barrier, inc=1, device_id={"ctx": lax.rem(me + d, ctx)}, device_id_type=MESH
        )
        return carry

    lax.fori_loop(1, ctx, greet_ctx, 0)
    greeted = ctx - 1
    quad_base = my_dp // QUAD * QUAD
    quad_at = my_dp - quad_base

    def quad_peer(d):
        return quad_base + lax.rem(quad_at + d, QUAD)

    def line_peer(d):
        return lax.rem(my_dp // QUAD + d, quads) * QUAD + quad_at

    if dp > 1:
        for d in range(1, QUAD):
            pl.semaphore_signal(barrier, inc=1, device_id={"dp": quad_peer(d)}, device_id_type=MESH)
        for d in range(1, quads):
            pl.semaphore_signal(barrier, inc=1, device_id={"dp": line_peer(d)}, device_id_type=MESH)
        greeted += QUAD - 1 + quads - 1

    def blank(slot):
        for g in range(KVH):
            kv[g, slot] = jnp.zeros((2, BLOCK, HD), jnp.bfloat16)

    @pl.when(me == 0)
    def _():
        blank(0)

    for k in range(1, BACK + 1):

        @pl.when(me <= k)
        def _():
            blank(OWN - k)

    mean = rew_ref[0, 0]
    for r in range(1, RESP):
        mean = mean + rew_ref[0, r]
    mean = mean * (1.0 / RESP)
    square = jnp.float32(0.0)
    advantage = jnp.float32(0.0)
    first = jnp.int32(1)
    start = jnp.int32(1)
    for r in range(RESP):
        centered = rew_ref[0, r] - mean
        square = square + centered * centered
        advantage = jnp.where(start <= me, centered, advantage)
        first = jnp.where(start <= me, start, first)
        start = start + len_ref[0, r]
    stat[0] = jnp.full((8, HD), square, jnp.float32)
    bias = [jnp.where(me >= 1, 0.0, MASKED).astype(jnp.float32)]
    for k in range(BACK, 0, -1):
        bias.append(jnp.where(me - k >= first, 0.0, MASKED).astype(jnp.float32))

    loads[0].wait()
    loads[1].wait()
    for g in range(KVH):
        kv[g, OWN, 0] = k_ref[:, g * HD : (g + 1) * HD]
        kv[g, OWN, 1] = v_ref[:, g * HD : (g + 1) * HD]

    pl.semaphore_wait(barrier, greeted)

    def remote(src, dst, send, recv, axis, target):
        return pltpu.make_async_remote_copy(
            src_ref=src,
            dst_ref=dst,
            send_sem=send,
            recv_sem=recv,
            device_id={axis: target},
            device_id_type=MESH,
        )

    def at(distance):
        return lax.rem(me + (distance + ctx), ctx)

    def begin(copy):
        copy.start()

    def left(copy):
        copy.wait_send()

    def key_copy(g, src_slot, dst_slot, send, distance):
        return remote(
            kv.at[g, src_slot], kv.at[g, dst_slot], send, frecv.at[g, dst_slot], "ctx", at(distance)
        )

    def arrive(g, slot):
        key_copy(g, OWN, slot, fsend.at[g, 0], 1).wait_recv()

    def sends(g):
        straight = g < OUT_STRAIGHT
        yield from ((me == 0, k, 0) for k in (1, 2, 3, COLS, 2 * COLS, 3 * COLS))
        yield (me >= 1) & (me + 1 < ctx), 1, OWN - 1
        yield (me >= 1) & (me + 4 < ctx), 4, OWN - 4
        yield (me >= 1) & (me + 3 < ctx), 3, OWN - 3
        yield (me >= 1) & (me + 2 < ctx) & straight, 2, OWN - 2

    def each_send(g, do):
        for n, (when, distance, slot) in enumerate(sends(g)):

            @pl.when(when)
            def _():
                do(key_copy(g, OWN, slot, fsend.at[g, n], distance))

    in_first = (me >= 1) & (me < COLS)
    line = lax.rem(me, COLS)
    if FORCED:
        pass_up = (me >= 2) & (line <= 2) & ((line == 2) | upward)
        pass_down = (me >= COLS + 1) & (line >= 1) & ((line == 1) | jnp.logical_not(upward))
        by_next = (line == COLS - 1) | ((line >= 1) & upward)
    else:
        pass_up = (me >= 2) & (me < end) & (upward | (me == end - 1))
        pass_down = (me >= COLS) & jnp.logical_not(upward)
        by_next = upward | (me == end)

    def each_prompt(g, do):
        @pl.when(in_first)
        def _():
            for n in range(3):
                do(key_copy(g, 0, 0, rsend.at[g, n], (n + 1) * COLS))

    passes = (
        (pass_up, OWN - 1, OWN - 2, 1, 3),
        (pass_down, OWN - 3, OWN - 2, -1, 4),
    )

    def each_pass(g, do, ready):
        for when, here, there, distance, n in passes:

            @pl.when(when)
            def _():
                if ready:
                    arrive(g, here)
                do(key_copy(g, here, there, rsend.at[g, n], distance))

    def relay_prompt(g):
        @pl.when(in_first)
        def _():
            arrive(g, 0)

        each_prompt(g, begin)

    def await_keys(g):
        @pl.when(me >= COLS)
        def _():
            arrive(g, 0)

        later = g >= OUT_STRAIGHT
        for k, passed in ((1, pass_up), (2, None), (3, pass_down), (4, None)):
            when = me > k
            if passed is not None:
                when = when & jnp.logical_not(passed & later)

            @pl.when(when)
            def _():
                arrive(g, OWN - k)

    def quad_copy(d):
        return remote(
            stat.at[0], quad_got.at[d - 1], qsend.at[d - 1], qrecv.at[d - 1], "dp", quad_peer(d)
        )

    def line_copy(d):
        return remote(
            stat.at[1], line_got.at[d - 1], lsend.at[d - 1], lrecv.at[d - 1], "dp", line_peer(d)
        )

    if dp > 1:
        for d in range(1, QUAD):
            quad_copy(d).start()
    each_send(0, begin)
    if dp > 1:
        for d in range(1, QUAD):
            quad_copy(d).wait()
        part = stat[0]
        for d in range(1, QUAD):
            part = part + quad_got[d - 1]
        stat[1] = part
    relay_prompt(0)
    for g in range(1, AHEAD):
        each_send(g, begin)
    if dp > 1:
        for d in range(1, quads):
            line_copy(d).start()
    loads[2].wait()
    loads[3].wait()

    def weigh():
        if dp > 1:
            for d in range(1, quads):
                line_copy(d).wait()
            total = stat[1]
            for d in range(1, quads):
                total = total + line_got[d - 1]
        else:
            total = stat[0]
        stat[2] = advantage / jnp.sqrt(total * (1.0 / (dp * RESP)) + 1e-06)

    def grad_copy(g, k):
        return remote(
            give.at[g, OWN - k], got.at[g, k - 1], gsend.at[g, k - 1], grecv.at[g, k - 1], "ctx", at(-k)
        )

    def help_copy(g, n):
        return remote(
            give.at[g, OWN - 2],
            help_got.at[g, n],
            hsend.at[g],
            hrecv.at[g, n],
            "ctx",
            at(1 if n else -1),
        )

    def chain_copy(g, n):
        return remote(
            give.at[g, 0], chain.at[g, n], csend.at[g], crecv.at[g, n], "ctx", at(-(n + 1) * COLS)
        )

    def home_copy(g, k):
        return remote(
            give.at[g, 0], got.at[g, k - 1], csend.at[g], grecv.at[g, k - 1], "ctx", at(-k)
        )

    def each_chain(g, do):
        for n in range(3):

            @pl.when((me >= (n + 1) * COLS) & (me < (n + 2) * COLS))
            def _():
                do(chain_copy(g, n))

    def each_home(g, do):
        for k in range(1, COLS):

            @pl.when(me == k)
            def _():
                do(home_copy(g, k))

    def give_next(g, do, when):
        @pl.when((me > 1) & when)
        def _():
            do(grad_copy(g, 1))

    def give_third(g, do, when):
        @pl.when((me > 3) & when)
        def _():
            do(grad_copy(g, 3))

    def give_fourth(g, do):
        @pl.when(me > 4)
        def _():
            do(grad_copy(g, 4))

    def give_second(g, do):
        @pl.when((me > 2) & back_straight(g))
        def _():
            do(grad_copy(g, 2))

        @pl.when((me > 2) & jnp.logical_not(back_straight(g)) & by_next)
        def _():
            do(help_copy(g, 0))

        @pl.when((me > 2) & jnp.logical_not(back_straight(g)) & jnp.logical_not(by_next))
        def _():
            do(help_copy(g, 1))

    def give_first(g):
        alone = back_straight(g)
        give_second(g, begin)
        give_next(g, begin, alone | jnp.logical_not(pass_up))
        give_third(g, begin, alone | jnp.logical_not(pass_down))
        each_chain(g, begin)
        give_fourth(g, begin)

    def back_straight(g):
        return g >= KVH - BACK_STRAIGHT

    def add_to_give(g, slot, parts):
        total = give[g, slot].astype(jnp.float32)
        for part in parts:
            total = total + part.astype(jnp.float32)
        give[g, slot] = total.astype(jnp.bfloat16)

    def assist(g):
        @pl.when(pass_up)
        def _():
            help_copy(g, 0).wait_recv()
            add_to_give(g, OWN - 1, [help_got[g, 0]])

        give_next(g, begin, pass_up)

        @pl.when(pass_down)
        def _():
            help_copy(g, 1).wait_recv()
            add_to_give(g, OWN - 3, [help_got[g, 1]])

        give_third(g, begin, pass_down)

    def assist_prompt(g):
        @pl.when(in_first)
        def _():
            for n in range(3):
                chain_copy(g, n).wait_recv()
            add_to_give(g, 0, [chain[g, n] for n in range(3)])

        each_home(g, begin)

    row = lax.broadcasted_iota(jnp.int32, (BLOCK, WIDE), 0)
    column = lax.broadcasted_iota(jnp.int32, (BLOCK, WIDE), 1)
    causal = row <= lax.rem(column, BLOCK)

    def pair_step(g, pair):
        base = pl.multiple_of(g * (RATIO * HD) + pair * WIDE, WIDE)
        left_half = pl.ds(base, HD)
        right_half = pl.ds(pl.multiple_of(base + HD, HD), HD)
        query = jnp.concatenate([q_ref[:, left_half], q_ref[:, right_half]], axis=0)
        cot = jnp.concatenate([c_ref[:, left_half], c_ref[:, right_half]], axis=0)
        keys = kv[g, :, 0].reshape(SLOTS * BLOCK, HD)
        values = kv[g, :, 1].reshape(SLOTS * BLOCK, HD)
        raw = dot(keys, query, NT) * (SCALE * LOG2E)
        tiles = [raw[s * BLOCK : (s + 1) * BLOCK] + bias[s] for s in range(OWN)]
        tiles.append(jnp.where(causal, raw[OWN * BLOCK :], MASKED))
        scores = jnp.concatenate(tiles, axis=0)
        peak = jnp.max(scores, axis=0, keepdims=True)
        exps = jnp.exp2(scores - peak)
        probs = exps * (1.0 / jnp.sum(exps, axis=0, keepdims=True))
        low = probs.astype(jnp.bfloat16)
        dprobs = dot(values, cot, NT)
        delta = jnp.sum(probs * dprobs, axis=0, keepdims=True)
        dscores = (probs * (dprobs - delta)).astype(jnp.bfloat16)
        attn = dot(vt[...], low)
        qgrad = dot(kt[...], dscores) * SCALE
        acc[0] += dot(dscores, query)
        acc[1] += dot(low, cot)
        o_ref[:, left_half] = attn[:, :HD].T.astype(jnp.bfloat16)
        o_ref[:, right_half] = attn[:, HD:].T.astype(jnp.bfloat16)
        dq_ref[:, left_half] = qgrad[:, :HD].T.astype(jnp.bfloat16)
        dq_ref[:, right_half] = qgrad[:, HD:].T.astype(jnp.bfloat16)

    def stores(g):
        heads = pl.ds(pl.multiple_of(g * (RATIO * HD), RATIO * HD), RATIO * HD)
        return [
            pltpu.make_async_copy(src.at[:, heads], dst.at[:, heads], store.at[g, n])
            for n, (src, dst) in enumerate(((o_ref, o_hbm), (dq_ref, dq_hbm)))
        ]

    def group_step(g, carry):
        await_keys(g)
        kt[...] = kv[g, :, 0].reshape(SLOTS * BLOCK, HD).T
        vt[...] = kv[g, :, 1].reshape(SLOTS * BLOCK, HD).T
        acc[...] = jnp.zeros_like(acc)

        def halves(half, inner):
            @pl.when((half == 0) & (g < KVH - AHEAD))
            def _():
                each_send(g + AHEAD, begin)

            @pl.when((half == 1) & (g < KVH - 1))
            def _():
                relay_prompt(g + 1)

            @pl.when((half == 1) & (g < KVH - 1) & (g + 1 >= OUT_STRAIGHT))
            def _():
                each_pass(g + 1, begin, True)

            @pl.when((half == 1) & (g > 0) & jnp.logical_not(back_straight(g - 1)))
            def _():
                assist(g - 1)

            @pl.when((half == 1) & (g > 0))
            def _():
                assist_prompt(g - 1)

            for n in range(PAIRS // 2):
                pair_step(g, half * (PAIRS // 2) + n)
            return inner

        lax.fori_loop(0, 2, halves, 0)

        @pl.when(g == 0)
        def _():
            weigh()

        weight = stat[2, 0:1, :]
        scale = weight * SCALE
        for s in range(OWN):
            rows = pl.ds(s * BLOCK, BLOCK)
            give[g, s, 0] = (acc[0, rows, :] * scale).astype(jnp.bfloat16)
            give[g, s, 1] = (acc[1, rows, :] * weight).astype(jnp.bfloat16)
        rows = pl.ds(OWN * BLOCK, BLOCK)
        own[g, 0] = acc[0, rows, :] * scale
        own[g, 1] = acc[1, rows, :] * weight
        give_first(g)
        for n in range(RATIO):
            head = pl.ds(pl.multiple_of(g * (RATIO * HD) + n * HD, HD), HD)
            dq_ref[:, head] = (dq_ref[:, head].astype(jnp.float32) * weight).astype(jnp.bfloat16)
        for copy in stores(g):
            copy.start()
        return carry

    lax.fori_loop(0, KVH, group_step, 0)
    assist_prompt(KVH - 1)

    def close_group(g, carry):
        def add(part):
            own[g] += part.astype(jnp.float32)

        for k in range(1, BACK + 1):
            here = (me >= 1) & (me + k < ctx)
            if k == 2:
                here = here & back_straight(g)
            if k < COLS:
                here = here | (me == 0)

            @pl.when(here)
            def _():
                grad_copy(g, k).wait_recv()
                add(got[g, k - 1])

        @pl.when(me == 0)
        def _():
            for n in range(3):
                chain_copy(g, n).wait_recv()
                add(chain[g, n])

        place = pl.ds(pl.multiple_of(g * HD, HD), HD)
        dk_ref[:, place] = own[g, 0].astype(jnp.bfloat16)
        dv_ref[:, place] = own[g, 1].astype(jnp.bfloat16)
        return carry

    lax.fori_loop(0, KVH, close_group, 0)

    def settle(g, carry):
        each_send(g, left)
        each_prompt(g, left)

        @pl.when(g >= OUT_STRAIGHT)
        def _():
            each_pass(g, left, False)

        for copy in stores(g):
            copy.wait()
        give_second(g, left)
        give_next(g, left, True)
        give_third(g, left, True)
        give_fourth(g, left)
        each_chain(g, left)
        each_home(g, left)
        return carry

    lax.fori_loop(0, KVH, settle, 0)


def place(*refs):
    sources, targets, parts, sems = refs[:4], refs[4:8], refs[8:12], refs[12]
    loads, stores = [], []
    for n in range(4):
        rows = BLOCK // 4 if n < 2 else BLOCK
        for c in range(BLOCK // rows):
            span = pl.ds(c * rows, rows)
            loads.append(
                pltpu.make_async_copy(sources[n].at[span], parts[n].at[span], sems.at[0, n, c])
            )
            stores.append(
                pltpu.make_async_copy(parts[n].at[span], targets[n].at[span], sems.at[1, n, c])
            )
    for copy in loads:
        copy.start()
    for load, store in zip(loads, stores):
        load.wait()
        store.start()
    for copy in stores:
        copy.wait()


def body(queries, keys, values, out_cotangent, rewards, lengths):
    ctx = lax.axis_size("ctx")
    dp = lax.axis_size("dp")
    tokens = queries.shape[1]
    vmem = pl.BlockSpec(memory_space=pltpu.VMEM)
    smem = pl.BlockSpec(memory_space=pltpu.SMEM)
    hbm = pl.BlockSpec(memory_space=pl.ANY)
    wide = jax.ShapeDtypeStruct((tokens, H * HD), jnp.bfloat16)
    thin = jax.ShapeDtypeStruct((tokens, KVH * HD), jnp.bfloat16)
    block = (2, BLOCK, HD)
    quads = max(dp // QUAD - 1, 1)
    dma = pltpu.SemaphoreType.DMA
    outs = pl.pallas_call(
        functools.partial(kernel, ctx, dp),
        out_shape=(wide, wide, thin, thin),
        in_specs=[hbm] * 4 + [smem] * 2,
        out_specs=(hbm, hbm, vmem, vmem),
        scratch_shapes=[
            pltpu.VMEM(wide.shape, jnp.bfloat16),
            pltpu.VMEM(wide.shape, jnp.bfloat16),
            pltpu.VMEM(wide.shape, jnp.bfloat16),
            pltpu.VMEM(wide.shape, jnp.bfloat16),
            pltpu.VMEM(thin.shape, jnp.bfloat16),
            pltpu.VMEM(thin.shape, jnp.bfloat16),
            pltpu.VMEM((KVH, SLOTS) + block, jnp.bfloat16),
            pltpu.VMEM((HD, SLOTS * BLOCK), jnp.bfloat16),
            pltpu.VMEM((HD, SLOTS * BLOCK), jnp.bfloat16),
            pltpu.VMEM((2, SLOTS * BLOCK, HD), jnp.float32),
            pltpu.VMEM((KVH,) + block, jnp.float32),
            pltpu.VMEM((KVH, OWN) + block, jnp.bfloat16),
            pltpu.VMEM((KVH, BACK) + block, jnp.bfloat16),
            pltpu.VMEM((KVH, 3) + block, jnp.bfloat16),
            pltpu.VMEM((KVH, 2) + block, jnp.bfloat16),
            pltpu.VMEM((3, 8, HD), jnp.float32),
            pltpu.VMEM((QUAD - 1, 8, HD), jnp.float32),
            pltpu.VMEM((quads, 8, HD), jnp.float32),
            dma((4,)),
            dma((KVH, 2)),
            dma((KVH, BACK + 6)),
            dma((KVH, SLOTS)),
            dma((KVH, 5)),
            dma((KVH, BACK)),
            dma((KVH, BACK)),
            dma((KVH,)),
            dma((KVH, 2)),
            dma((KVH,)),
            dma((KVH, 3)),
            dma((QUAD - 1,)),
            dma((QUAD - 1,)),
            dma((quads,)),
            dma((quads,)),
        ],
        compiler_params=pltpu.CompilerParams(
            collective_id=0, has_side_effects=True, vmem_limit_bytes=61 * 1024 * 1024
        ),
        name="tree_attention",
    )(queries[0], out_cotangent[0], keys[0], values[0], rewards, lengths)
    outs = pl.pallas_call(
        place,
        out_shape=(wide, wide, thin, thin),
        in_specs=[hbm] * 4,
        out_specs=(hbm,) * 4,
        scratch_shapes=[pltpu.VMEM(out.shape, out.dtype) for out in (wide, wide, thin, thin)]
        + [dma((2, 4, 4))],
        compiler_params=pltpu.CompilerParams(vmem_limit_bytes=61 * 1024 * 1024),
        name="place_results",
    )(*outs)
    return tuple(out[None] for out in outs)


def solution(mesh):
    placed = (P("dp", "ctx", None),) * 4
    return jax.shard_map(
        body,
        mesh=mesh,
        in_specs=placed + (P("dp", None),) * 2,
        out_specs=placed,
        check_vma=False,
    )
```

```python
import functools

import jax
import jax.numpy as jnp
from jax import lax
from jax.experimental import pallas as pl
from jax.experimental.pallas import tpu as pltpu
from jax.sharding import PartitionSpec as P

H = 32
KVH = 4
HD = 128
BLOCK = 128
RESP = 6
BACK = 4
SLOTS = BACK + 2
OWN = SLOTS - 1
COLS = 4
QUAD = 4
RATIO = H // KVH
PAIRS = RATIO // 2
WIDE = 2 * BLOCK
SCALE = HD ** (-0.5)
LOG2E = 1.4426950408889634
MASKED = -1e30
SEND_ORDER = (1, 4, 3, 2)
BACK_ORDER = (2, 1, 3, 4)
MESH = pl.DeviceIdType.MESH
NT = (((1,), (1,)), ((), ()))
NN = (((1,), (0,)), ((), ()))


def dot(a, b, dims=NN):
    return lax.dot_general(a, b, dims, preferred_element_type=jnp.float32)


def kernel(
    ctx,
    dp,
    q_hbm,
    c_hbm,
    k_hbm,
    v_hbm,
    rew_ref,
    len_ref,
    o_hbm,
    dq_hbm,
    dk_ref,
    dv_ref,
    o_ref,
    dq_ref,
    q_ref,
    c_ref,
    k_ref,
    v_ref,
    kv,
    kt,
    vt,
    acc,
    own,
    give,
    got,
    chain,
    stat,
    quad_got,
    line_got,
    load,
    store,
    fsend,
    frecv,
    rsend,
    gsend,
    grecv,
    csend,
    crecv,
    qsend,
    qrecv,
    lsend,
    lrecv,
):
    me = lax.axis_index("ctx")
    end = ctx - 1
    my_dp = lax.axis_index("dp")
    quads = dp // QUAD

    loads = [
        pltpu.make_async_copy(src, dst, load.at[n])
        for n, (src, dst) in enumerate(
            ((k_hbm, k_ref), (v_hbm, v_ref), (q_hbm, q_ref), (c_hbm, c_ref))
        )
    ]
    for copy in loads:
        copy.start()

    barrier = pltpu.get_barrier_semaphore()

    def greet_ctx(d, carry):
        pl.semaphore_signal(
            barrier, inc=1, device_id={"ctx": lax.rem(me + d, ctx)}, device_id_type=MESH
        )
        return carry

    lax.fori_loop(1, ctx, greet_ctx, 0)
    greeted = ctx - 1
    quad_base = my_dp // QUAD * QUAD
    quad_at = my_dp - quad_base

    def quad_peer(d):
        return quad_base + lax.rem(quad_at + d, QUAD)

    def line_peer(d):
        return lax.rem(my_dp // QUAD + d, quads) * QUAD + quad_at

    if dp > 1:
        for d in range(1, QUAD):
            pl.semaphore_signal(barrier, inc=1, device_id={"dp": quad_peer(d)}, device_id_type=MESH)
        for d in range(1, quads):
            pl.semaphore_signal(barrier, inc=1, device_id={"dp": line_peer(d)}, device_id_type=MESH)
        greeted += QUAD - 1 + quads - 1

    def blank(slot):
        for g in range(KVH):
            kv[g, slot] = jnp.zeros((2, BLOCK, HD), jnp.bfloat16)

    @pl.when(me == 0)
    def _():
        blank(0)

    for k in range(1, BACK + 1):

        @pl.when(me <= k)
        def _():
            blank(OWN - k)

    mean = rew_ref[0, 0]
    for r in range(1, RESP):
        mean = mean + rew_ref[0, r]
    mean = mean * (1.0 / RESP)
    square = jnp.float32(0.0)
    advantage = jnp.float32(0.0)
    first = jnp.int32(1)
    start = jnp.int32(1)
    for r in range(RESP):
        centered = rew_ref[0, r] - mean
        square = square + centered * centered
        advantage = jnp.where(start <= me, centered, advantage)
        first = jnp.where(start <= me, start, first)
        start = start + len_ref[0, r]
    stat[0] = jnp.full((8, HD), square, jnp.float32)
    bias = [jnp.where(me >= 1, 0.0, MASKED).astype(jnp.float32)]
    for k in range(BACK, 0, -1):
        bias.append(jnp.where(me - k >= first, 0.0, MASKED).astype(jnp.float32))

    loads[0].wait()
    loads[1].wait()
    for g in range(KVH):
        kv[g, OWN, 0] = k_ref[:, g * HD : (g + 1) * HD]
        kv[g, OWN, 1] = v_ref[:, g * HD : (g + 1) * HD]

    pl.semaphore_wait(barrier, greeted)

    def remote(src, dst, send, recv, axis, target):
        return pltpu.make_async_remote_copy(
            src_ref=src,
            dst_ref=dst,
            send_sem=send,
            recv_sem=recv,
            device_id={axis: target},
            device_id_type=MESH,
        )

    def at(distance):
        return lax.rem(me + (distance + ctx), ctx)

    def begin(copy):
        copy.start()

    def left(copy):
        copy.wait_send()

    def key_copy(g, src_slot, dst_slot, send, distance):
        return remote(
            kv.at[g, src_slot], kv.at[g, dst_slot], send, frecv.at[g, dst_slot], "ctx", at(distance)
        )

    def arrive(g, slot):
        key_copy(g, OWN, slot, fsend.at[g, 0], 1).wait_recv()

    def sends(g):
        yield from ((me == 0, k, 0) for k in (1, 2, 3, COLS, 2 * COLS, 3 * COLS))
        for k in SEND_ORDER:
            when = (me >= 1) & (me + k < ctx)
            yield when, k, OWN - k

    def each_send(g, do):
        for n, (when, distance, slot) in enumerate(sends(g)):

            @pl.when(when)
            def _():
                do(key_copy(g, OWN, slot, fsend.at[g, n], distance))

    in_first = (me >= 1) & (me < COLS)

    def each_prompt(g, do):
        @pl.when(in_first)
        def _():
            for n in range(3):
                do(key_copy(g, 0, 0, rsend.at[g, n], (n + 1) * COLS))

    def relay_prompt(g):
        @pl.when(in_first)
        def _():
            arrive(g, 0)

        each_prompt(g, begin)

    def await_keys(g):
        @pl.when(me >= COLS)
        def _():
            arrive(g, 0)

        for k in range(1, BACK + 1):
            when = me > k
            @pl.when(when)
            def _():
                arrive(g, OWN - k)

    def quad_copy(d):
        return remote(
            stat.at[0], quad_got.at[d - 1], qsend.at[d - 1], qrecv.at[d - 1], "dp", quad_peer(d)
        )

    def line_copy(d):
        return remote(
            stat.at[1], line_got.at[d - 1], lsend.at[d - 1], lrecv.at[d - 1], "dp", line_peer(d)
        )

    if dp > 1:
        for d in range(1, QUAD):
            quad_copy(d).start()
    each_send(0, begin)
    if dp > 1:
        for d in range(1, QUAD):
            quad_copy(d).wait()
        part = stat[0]
        for d in range(1, QUAD):
            part = part + quad_got[d - 1]
        stat[1] = part
    relay_prompt(0)
    for g in range(1, KVH):
        each_send(g, begin)
    if dp > 1:
        for d in range(1, quads):
            line_copy(d).start()
    loads[2].wait()
    loads[3].wait()

    def weigh():
        if dp > 1:
            for d in range(1, quads):
                line_copy(d).wait()
            total = stat[1]
            for d in range(1, quads):
                total = total + line_got[d - 1]
        else:
            total = stat[0]
        stat[2] = advantage / jnp.sqrt(total * (1.0 / (dp * RESP)) + 1e-06)

    def grad_copy(g, k):
        return remote(
            give.at[g, OWN - k], got.at[g, k - 1], gsend.at[g, k - 1], grecv.at[g, k - 1], "ctx", at(-k)
        )

    def chain_copy(g, n):
        return remote(
            give.at[g, 0], chain.at[g, n], csend.at[g], crecv.at[g, n], "ctx", at(-(n + 1) * COLS)
        )

    def home_copy(g, k):
        return remote(
            give.at[g, 0], got.at[g, k - 1], csend.at[g], grecv.at[g, k - 1], "ctx", at(-k)
        )

    def each_chain(g, do):
        for n in range(3):

            @pl.when((me >= (n + 1) * COLS) & (me < (n + 2) * COLS))
            def _():
                do(chain_copy(g, n))

    def each_home(g, do):
        for k in range(1, COLS):

            @pl.when(me == k)
            def _():
                do(home_copy(g, k))

    def each_grad(g, do):
        for k in BACK_ORDER:

            @pl.when(me > k)
            def _():
                do(grad_copy(g, k))

    def give_first(g):
        each_chain(g, begin)
        each_grad(g, begin)

    def add_to_give(g, slot, parts):
        total = give[g, slot].astype(jnp.float32)
        for part in parts:
            total = total + part.astype(jnp.float32)
        give[g, slot] = total.astype(jnp.bfloat16)

    def assist_prompt(g):
        @pl.when(in_first)
        def _():
            for n in range(3):
                chain_copy(g, n).wait_recv()
            add_to_give(g, 0, [chain[g, n] for n in range(3)])

        each_home(g, begin)

    row = lax.broadcasted_iota(jnp.int32, (BLOCK, WIDE), 0)
    column = lax.broadcasted_iota(jnp.int32, (BLOCK, WIDE), 1)
    causal = row <= lax.rem(column, BLOCK)

    def pair_step(g, pair):
        base = pl.multiple_of(g * (RATIO * HD) + pair * WIDE, WIDE)
        left_half = pl.ds(base, HD)
        right_half = pl.ds(pl.multiple_of(base + HD, HD), HD)
        query = jnp.concatenate([q_ref[:, left_half], q_ref[:, right_half]], axis=0)
        cot = jnp.concatenate([c_ref[:, left_half], c_ref[:, right_half]], axis=0)
        keys = kv[g, :, 0].reshape(SLOTS * BLOCK, HD)
        values = kv[g, :, 1].reshape(SLOTS * BLOCK, HD)
        raw = dot(keys, query, NT) * (SCALE * LOG2E)
        tiles = [raw[s * BLOCK : (s + 1) * BLOCK] + bias[s] for s in range(OWN)]
        tiles.append(jnp.where(causal, raw[OWN * BLOCK :], MASKED))
        scores = jnp.concatenate(tiles, axis=0)
        peak = jnp.max(scores, axis=0, keepdims=True)
        exps = jnp.exp2(scores - peak)
        probs = exps * (1.0 / jnp.sum(exps, axis=0, keepdims=True))
        low = probs.astype(jnp.bfloat16)
        dprobs = dot(values, cot, NT)
        delta = jnp.sum(probs * dprobs, axis=0, keepdims=True)
        dscores = (probs * (dprobs - delta)).astype(jnp.bfloat16)
        attn = dot(vt[...], low)
        qgrad = dot(kt[...], dscores) * SCALE
        acc[0] += dot(dscores, query)
        acc[1] += dot(low, cot)
        o_ref[:, left_half] = attn[:, :HD].T.astype(jnp.bfloat16)
        o_ref[:, right_half] = attn[:, HD:].T.astype(jnp.bfloat16)
        dq_ref[:, left_half] = qgrad[:, :HD].T.astype(jnp.bfloat16)
        dq_ref[:, right_half] = qgrad[:, HD:].T.astype(jnp.bfloat16)

    def stores(g):
        heads = pl.ds(pl.multiple_of(g * (RATIO * HD), RATIO * HD), RATIO * HD)
        return [
            pltpu.make_async_copy(src.at[:, heads], dst.at[:, heads], store.at[g, n])
            for n, (src, dst) in enumerate(((o_ref, o_hbm), (dq_ref, dq_hbm)))
        ]

    def group_step(g, carry):
        await_keys(g)
        kt[...] = kv[g, :, 0].reshape(SLOTS * BLOCK, HD).T
        vt[...] = kv[g, :, 1].reshape(SLOTS * BLOCK, HD).T
        acc[...] = jnp.zeros_like(acc)

        for n in range(PAIRS):
            pair_step(g, n)

        @pl.when(g < KVH - 1)
        def _():
            relay_prompt(g + 1)

        @pl.when(g > 0)
        def _():
            assist_prompt(g - 1)

        @pl.when(g == 0)
        def _():
            weigh()

        weight = stat[2, 0:1, :]
        scale = weight * SCALE
        for s in range(OWN):
            rows = pl.ds(s * BLOCK, BLOCK)
            give[g, s, 0] = (acc[0, rows, :] * scale).astype(jnp.bfloat16)
            give[g, s, 1] = (acc[1, rows, :] * weight).astype(jnp.bfloat16)
        rows = pl.ds(OWN * BLOCK, BLOCK)
        own[g, 0] = acc[0, rows, :] * scale
        own[g, 1] = acc[1, rows, :] * weight
        give_first(g)
        for n in range(RATIO):
            head = pl.ds(pl.multiple_of(g * (RATIO * HD) + n * HD, HD), HD)
            dq_ref[:, head] = (dq_ref[:, head].astype(jnp.float32) * weight).astype(jnp.bfloat16)
        for copy in stores(g):
            copy.start()
        return carry

    lax.fori_loop(0, KVH, group_step, 0)
    assist_prompt(KVH - 1)

    def close_group(g, carry):
        def add(part):
            own[g] += part.astype(jnp.float32)

        for k in range(1, BACK + 1):
            here = (me >= 1) & (me + k < ctx)
            if k < COLS:
                here = here | (me == 0)

            @pl.when(here)
            def _():
                grad_copy(g, k).wait_recv()
                add(got[g, k - 1])

        @pl.when(me == 0)
        def _():
            for n in range(3):
                chain_copy(g, n).wait_recv()
                add(chain[g, n])

        place = pl.ds(pl.multiple_of(g * HD, HD), HD)
        dk_ref[:, place] = own[g, 0].astype(jnp.bfloat16)
        dv_ref[:, place] = own[g, 1].astype(jnp.bfloat16)
        return carry

    lax.fori_loop(0, KVH, close_group, 0)

    def settle(g, carry):
        each_send(g, left)
        each_prompt(g, left)

        for copy in stores(g):
            copy.wait()
        each_grad(g, left)
        each_chain(g, left)
        each_home(g, left)
        return carry

    lax.fori_loop(0, KVH, settle, 0)


def place(*refs):
    sources, targets, parts, sems = refs[:4], refs[4:8], refs[8:12], refs[12]
    loads, stores = [], []
    for n in range(4):
        rows = BLOCK // 4 if n < 2 else BLOCK
        for c in range(BLOCK // rows):
            span = pl.ds(c * rows, rows)
            loads.append(
                pltpu.make_async_copy(sources[n].at[span], parts[n].at[span], sems.at[0, n, c])
            )
            stores.append(
                pltpu.make_async_copy(parts[n].at[span], targets[n].at[span], sems.at[1, n, c])
            )
    for copy in loads:
        copy.start()
    for load, store in zip(loads, stores):
        load.wait()
        store.start()
    for copy in stores:
        copy.wait()


def body(queries, keys, values, out_cotangent, rewards, lengths):
    ctx = lax.axis_size("ctx")
    dp = lax.axis_size("dp")
    tokens = queries.shape[1]
    vmem = pl.BlockSpec(memory_space=pltpu.VMEM)
    smem = pl.BlockSpec(memory_space=pltpu.SMEM)
    hbm = pl.BlockSpec(memory_space=pl.ANY)
    wide = jax.ShapeDtypeStruct((tokens, H * HD), jnp.bfloat16)
    thin = jax.ShapeDtypeStruct((tokens, KVH * HD), jnp.bfloat16)
    block = (2, BLOCK, HD)
    quads = max(dp // QUAD - 1, 1)
    dma = pltpu.SemaphoreType.DMA
    outs = pl.pallas_call(
        functools.partial(kernel, ctx, dp),
        out_shape=(wide, wide, thin, thin),
        in_specs=[hbm] * 4 + [smem] * 2,
        out_specs=(hbm, hbm, vmem, vmem),
        scratch_shapes=[
            pltpu.VMEM(wide.shape, jnp.bfloat16),
            pltpu.VMEM(wide.shape, jnp.bfloat16),
            pltpu.VMEM(wide.shape, jnp.bfloat16),
            pltpu.VMEM(wide.shape, jnp.bfloat16),
            pltpu.VMEM(thin.shape, jnp.bfloat16),
            pltpu.VMEM(thin.shape, jnp.bfloat16),
            pltpu.VMEM((KVH, SLOTS) + block, jnp.bfloat16),
            pltpu.VMEM((HD, SLOTS * BLOCK), jnp.bfloat16),
            pltpu.VMEM((HD, SLOTS * BLOCK), jnp.bfloat16),
            pltpu.VMEM((2, SLOTS * BLOCK, HD), jnp.float32),
            pltpu.VMEM((KVH,) + block, jnp.float32),
            pltpu.VMEM((KVH, OWN) + block, jnp.bfloat16),
            pltpu.VMEM((KVH, BACK) + block, jnp.bfloat16),
            pltpu.VMEM((KVH, 3) + block, jnp.bfloat16),
            pltpu.VMEM((3, 8, HD), jnp.float32),
            pltpu.VMEM((QUAD - 1, 8, HD), jnp.float32),
            pltpu.VMEM((quads, 8, HD), jnp.float32),
            dma((4,)),
            dma((KVH, 2)),
            dma((KVH, BACK + 6)),
            dma((KVH, SLOTS)),
            dma((KVH, 3)),
            dma((KVH, BACK)),
            dma((KVH, BACK)),
            dma((KVH,)),
            dma((KVH, 3)),
            dma((QUAD - 1,)),
            dma((QUAD - 1,)),
            dma((quads,)),
            dma((quads,)),
        ],
        compiler_params=pltpu.CompilerParams(
            collective_id=0, has_side_effects=True, vmem_limit_bytes=61 * 1024 * 1024
        ),
        name="tree_attention",
    )(queries[0], out_cotangent[0], keys[0], values[0], rewards, lengths)
    outs = pl.pallas_call(
        place,
        out_shape=(wide, wide, thin, thin),
        in_specs=[hbm] * 4,
        out_specs=(hbm,) * 4,
        scratch_shapes=[pltpu.VMEM(out.shape, out.dtype) for out in (wide, wide, thin, thin)]
        + [dma((2, 4, 4))],
        compiler_params=pltpu.CompilerParams(vmem_limit_bytes=61 * 1024 * 1024),
        name="place_results",
    )(*outs)
    return tuple(out[None] for out in outs)


def solution(mesh):
    placed = (P("dp", "ctx", None),) * 4
    return jax.shard_map(
        body,
        mesh=mesh,
        in_specs=placed + (P("dp", None),) * 2,
        out_specs=placed,
        check_vma=False,
    )
```
